768 devices in a mesh: row: 8 (over y_lo, x), rep: 96 (over y_hi, z, core).
Axes of the slice: x: 4, y: 8 (y_hi: 4, y_lo: 2; y = y_hi * 2 + y_lo), z: 12, core: 2. Of those that a mesh axis runs over, the one named last changes fastest.
Arguments:
- features: bfloat16 [196608, 256], P(('row', 'rep')), may hold values from -6 to 6
- weight: bfloat16 [256, 256], replicated, may hold values from -0.375 to 0.375
- bias: float32 [256], replicated, may hold values from -3 to 3
- tile_vals: bfloat16 [8, 96, 32, 128, 128], P('row', 'rep'), may hold values from -0.25 to 0.25
- tile_rows: int32 [8, 96, 32], P('row', 'rep'), may hold values from 0 to 15, as said below
- tile_cols: int32 [8, 96, 32], P('row', 'rep'), may hold values from 0 to 15, as said below
- tile_counts: int32 [8, 96], P('row', 'rep'), may hold values from 1 to 32, as said below
- grad_out: bfloat16 [196608, 256], P(('row', 'rep')), may hold values from -6 to 6
Outputs:
- activations: bfloat16 [196608, 256], P(('row', 'rep'))
- grad_features: bfloat16 [196608, 256], P(('row', 'rep'))
- grad_weight: float32 [256, 256], replicated
- grad_bias: float32 [256], replicated
The draws below stay inside these ranges and needn't reach their ends.
Inputs may be any that keep to these rules, and one draw needn't show every extreme that they name: `tile_rows`: destination tile indices; within one device the first tile_counts slots name distinct (tile_rows, tile_cols) pairs, and slots at or past tile_counts are unused. `tile_cols`: source tile indices. `tile_counts`: live slots per device; some device has all 32 slots live.
All inputs are finite; a program needn't handle non-finite values.
Results may differ from the reference program's by a relative error of at most 0.013.
Values may be sent and summed in bfloat16 or wider, within the bound.
No kernel may reach another device: no remote copies, remote signals or barrier semaphores. Data moves between devices by JAX's collectives and lax.ppermute only.
A program may use at most 32 MiB of HBM per device.

```python
import jax
import jax.numpy as jnp
from jax import lax

H = 256
TILE = 128
BLOCK_TILES = 2
K = 8
MAXT = 32
NODES = 196608
N_ROW = 8
N_REP = 96


def tile_layout(key):
    first, second, third, fourth = jax.random.split(key, 4)
    count_all = N_ROW * N_REP
    left = jax.random.randint(first, (count_all,), 0, MAXT)
    right = jax.random.randint(second, (count_all,), 0, MAXT)
    counts = 1 + left * right // MAXT
    fullest = jax.random.randint(third, (), 0, count_all)
    counts = counts.at[fullest].set(MAXT)
    grid_size = K * BLOCK_TILES * N_ROW * BLOCK_TILES
    keys = jax.random.split(fourth, count_all)
    places = jax.vmap(lambda one: jax.random.permutation(one, grid_size))(keys)[:, :MAXT]
    places = places.astype(jnp.int32)
    across = N_ROW * BLOCK_TILES
    rows = (places // across).reshape(N_ROW, N_REP, MAXT)
    cols = (places % across).reshape(N_ROW, N_REP, MAXT)
    return (rows, cols, counts.reshape(N_ROW, N_REP).astype(jnp.int32))


def draw_tile_rows(key, part):
    return tile_layout(key)[0]


def draw_tile_cols(key, part):
    return tile_layout(key)[1]


def draw_tile_counts(key, part):
    return tile_layout(key)[2]


def block_scale(key, dims, shards, low, high):
    level = 1.0
    for dim, blocks in shards:
        heights = jax.random.uniform(jax.random.fold_in(jax.random.fold_in(key, 6), dim), (blocks,), jnp.float32, low / len(shards), high / len(shards))
        level = level * jnp.repeat(jnp.exp(heights), dims[dim] // blocks).reshape((-1,) + (1,) * (len(dims) - 1 - dim))
    return level


def noise(rng, shape, width, most, cuts=(), kind=jnp.bfloat16):
    entries = width * jax.random.normal(rng, shape, jnp.float32)
    if cuts:
        entries = entries * block_scale(rng, shape, cuts, -0.22, 0.18)
    return jnp.clip(entries, -most, most).astype(kind)


def setup_inputs(seed: int = 0) -> dict:
    splits = jax.random.split(jax.random.key(seed), 9)
    return {
        "features": noise(splits[0], (NODES, H), 1.0, 6.0, ((0, 768),)),
        "weight": noise(splits[1], (H, H), H ** -0.5, 0.375),
        "bias": noise(splits[2], (H,), 0.5, 3.0, (), jnp.float32),
        "tile_vals": noise(splits[3], (N_ROW, N_REP, MAXT, TILE, TILE), (TILE * 4) ** -0.5, 0.25, ((0, 8), (1, 96))),
        "tile_rows": draw_tile_rows(jax.random.fold_in(splits[8], 71), 0),
        "tile_cols": draw_tile_cols(jax.random.fold_in(splits[8], 71), 0),
        "tile_counts": draw_tile_counts(jax.random.fold_in(splits[8], 71), 0),
        "grad_out": noise(splits[7], (NODES, H), 1.0, 6.0, ((0, 768),)),
    }


def reference(features, weight, bias, tile_vals, tile_rows, tile_cols, tile_counts, grad_out):
    block = TILE * BLOCK_TILES
    xw = jnp.dot(features, weight, preferred_element_type=jnp.float32).astype(jnp.bfloat16)
    xw_blocks = xw.reshape(N_ROW, N_REP, block, H)
    slots = jnp.arange(MAXT, dtype=jnp.int32)
    offsets = jnp.arange(K, dtype=jnp.int32)

    def forward(carry, index):
        r = index // N_REP
        p = index % N_REP
        vals = tile_vals[r, p].astype(jnp.float32)
        live = (slots < tile_counts[r, p]).astype(jnp.float32)
        source = xw_blocks[:, p].reshape(N_ROW * BLOCK_TILES, TILE, H).astype(jnp.float32)[tile_cols[r, p]]
        product = jnp.einsum('tij,tjh->tih', vals, source) * live[:, None, None]
        part = jnp.zeros((K * BLOCK_TILES, TILE, H), jnp.float32).at[tile_rows[r, p]].add(product)
        targets = (p + offsets) % N_REP
        carry = carry.at[r, targets].add(part.reshape(K, block, H))
        return carry, None

    aggregate = lax.scan(forward, jnp.zeros((N_ROW, N_REP, block, H), jnp.float32),
                         jnp.arange(N_ROW * N_REP, dtype=jnp.int32))[0]
    pre = aggregate.reshape(NODES, H) + bias[None, :]
    activations = jax.nn.silu(pre).astype(jnp.bfloat16)
    sig = jax.nn.sigmoid(pre)
    grad_pre = (grad_out.astype(jnp.float32) * sig * (1.0 + pre * (1.0 - sig))).astype(jnp.bfloat16)
    grad_blocks = grad_pre.reshape(N_ROW, N_REP, block, H)

    def backward(carry, index):
        r = index // N_REP
        p = index % N_REP
        vals = tile_vals[r, p].astype(jnp.float32)
        live = (slots < tile_counts[r, p]).astype(jnp.float32)
        targets = (p + offsets) % N_REP
        dest = grad_blocks[r, targets].reshape(K * BLOCK_TILES, TILE, H).astype(jnp.float32)[tile_rows[r, p]]
        product = jnp.einsum('tij,tih->tjh', vals, dest) * live[:, None, None]
        part = jnp.zeros((N_ROW * BLOCK_TILES, TILE, H), jnp.float32).at[tile_cols[r, p]].add(product)
        carry = carry.at[:, p].add(part.reshape(N_ROW, block, H))
        return carry, None

    source = lax.scan(backward, jnp.zeros((N_ROW, N_REP, block, H), jnp.float32),
                      jnp.arange(N_ROW * N_REP, dtype=jnp.int32))[0]
    source_grad = source.reshape(NODES, H).astype(jnp.bfloat16)
    grad_features = jnp.dot(source_grad, weight.T, preferred_element_type=jnp.float32).astype(jnp.bfloat16)
    grad_weight = jnp.dot(features.T, source_grad, preferred_element_type=jnp.float32)
    grad_bias = jnp.sum(grad_pre.astype(jnp.float32), axis=0)
    return activations, grad_features, grad_weight, grad_bias
```

```python
import jax
import jax.numpy as jnp
from jax import lax
from jax.experimental import pallas as pl
from jax.experimental.pallas import tpu as pltpu
from jax.sharding import PartitionSpec as P

K = 8
BF = jnp.bfloat16
F32 = jnp.float32


def forward_tiles(rows, cols, count, vals, source, even, odd, acc):
    acc[...] = jnp.zeros_like(acc)
    live = count[0]
    for t in range(vals.shape[0]):
        product = jnp.dot(vals[t], source[cols[t]], preferred_element_type=F32)
        acc[rows[t]] += jnp.where(t < live, product, 0.0)
    tile = vals.shape[1]
    for o in range(K):
        for h in range(2):
            part = acc[2 * o + h].astype(BF)
            target = odd if o % 2 else even
            target[o // 2, h * tile : (h + 1) * tile, :] = part


def backward_tiles(rows, cols, count, vals, even, odd, out, acc):
    acc[...] = jnp.zeros_like(acc)
    live = count[0]
    for t in range(vals.shape[0]):
        row = rows[t]
        place = (row // 4) * 2 + row % 2
        reached = jnp.where(row % 4 >= 2, odd[place], even[place])
        product = lax.dot_general(
            vals[t], reached, (((0,), (0,)), ((), ())), preferred_element_type=F32
        )
        acc[cols[t]] += jnp.where(t < live, product, 0.0)
    out[...] = acc[...].astype(BF)


def tiles_call(kernel, rows, cols, count, vals, arrays, outs):
    slots, tile = vals.shape[0], vals.shape[1]
    width = arrays[0].shape[-1]
    smem = pl.BlockSpec(memory_space=pltpu.SMEM)
    vmem = pl.BlockSpec(memory_space=pltpu.VMEM)
    return pl.pallas_call(
        kernel,
        out_shape=outs,
        in_specs=[smem] * 3 + [vmem] * (1 + len(arrays)),
        out_specs=jax.tree.map(lambda _: vmem, outs),
        scratch_shapes=[pltpu.VMEM((2 * K, tile, width), F32)],
        compiler_params=pltpu.CompilerParams(vmem_limit_bytes=24 * 1024 * 1024),
        cost_estimate=pl.CostEstimate(
            flops=2 * slots * tile * tile * width, bytes_accessed=3 << 20, transcendentals=0
        ),
    )(rows, cols, count, vals, *arrays)


def passed(shard, axis, to):
    size = lax.axis_size(axis)
    pairs = [(i, to(i)) for i in range(size)]
    return lax.ppermute(shard, axis, [(i, j % size) for i, j in pairs if j is not None])


def gathered(shard, axis, groups=None):
    size = lax.axis_size(axis) if groups is None else len(groups[0])
    copies = jnp.broadcast_to(shard[None], (size,) + shard.shape)
    return lax.all_to_all(copies, axis, 0, 0, axis_index_groups=groups)


def total_over_mesh(local_weight, local_bias, z_chips):
    reps = lax.axis_size("rep")
    rows = lax.axis_size("row")
    width = local_weight.shape[1]
    core = lax.axis_index("rep") % 2
    half = local_weight.shape[0] // 2
    piece = half // rows
    give = jnp.where(core == 0, local_weight[half:], local_weight[:half])
    keep = jnp.where(core == 0, local_weight[:half], local_weight[half:])
    bias = jnp.broadcast_to(local_bias[None, None], (rows, 1, width))
    pad = jnp.zeros((rows, 15, width), BF)

    weight = keep + passed(give, "rep", lambda i: i ^ 1).astype(F32)
    parts = jnp.concatenate(
        [weight.reshape(rows, piece, width).astype(BF), bias.astype(BF), pad], axis=1
    )
    summed = jnp.sum(lax.all_to_all(parts, "row", 0, 0).astype(F32), axis=0).astype(BF)
    line = [
        [y * 2 * z_chips + 2 * z + c for z in range(z_chips)]
        for y in range(reps // (2 * z_chips))
        for c in range(2)
    ]
    summed = jnp.sum(gathered(summed, "rep", line).astype(F32), axis=0).astype(BF)
    across = [
        [y * 2 * z_chips + i for y in range(reps // (2 * z_chips))] for i in range(2 * z_chips)
    ]
    summed = jnp.sum(gathered(summed, "rep", across).astype(F32), axis=0)
    other = passed(summed, "rep", lambda i: i ^ 1)
    low = jnp.where(core == 0, summed, other)
    high = jnp.where(core == 0, other, summed)
    bias_sum = (low + high)[piece]
    both = jnp.stack([low[:piece], high[:piece]])
    everything = gathered(both, "row")
    weight_sum = jnp.swapaxes(everything, 0, 1).reshape(2 * half, width)
    return weight_sum, bias_sum


def shards(features, weight, bias, tile_vals, tile_rows, tile_cols, tile_counts, grad_out):
    block, width = features.shape
    vals = tile_vals[0, 0]
    rows = tile_rows[0, 0]
    cols = tile_cols[0, 0]
    count = tile_counts[0]
    tile = vals.shape[1]
    group_rows = lax.axis_size("row")
    core = lax.axis_index("rep") % 2
    wide = jax.ShapeDtypeStruct((K // 2, block, width), BF)

    with jax.named_scope("gather_features"):
        source = gathered(features, "row").reshape(group_rows * block // tile, tile, width)
    with jax.named_scope("forward_tiles"):
        even, odd = tiles_call(
            forward_tiles, rows, cols, count, vals, [source], (wide, wide)
        )
    with jax.named_scope("window_sum"):
        far = passed(odd[3], "rep", lambda i: i + 7 if i % 2 else None)
        other = passed(odd, "rep", lambda i: i ^ 1)
        shifted = jnp.concatenate([jnp.zeros_like(other[:1]), other[:3]])
        sums = even.astype(F32) + jnp.where(core == 0, shifted, other).astype(F32)
        near = passed(jnp.stack([sums[1], sums[3]]).astype(BF), "rep", lambda i: i + 2)
        middle = passed((sums[2] + near[1].astype(F32)).astype(BF), "rep", lambda i: i + 4)
        aggregate = sums[0] + near[0].astype(F32) + far.astype(F32) + middle.astype(F32)
    with jax.named_scope("pointwise"):
        top = aggregate.astype(BF)
        rest = (aggregate - top.astype(F32)).astype(BF)
        pre = (
            jnp.dot(top, weight, preferred_element_type=F32)
            + jnp.dot(rest, weight, preferred_element_type=F32)
            + bias[None, :]
        )
        activations = jax.nn.silu(pre).astype(BF)
        sig = jax.nn.sigmoid(pre)
        grad_pre = (grad_out.astype(F32) * sig * (1.0 + pre * (1.0 - sig))).astype(BF)
        local_weight = lax.dot_general(
            top, grad_pre, (((0,), (0,)), ((), ())), preferred_element_type=F32
        )
        local_bias = jnp.sum(grad_pre.astype(F32), axis=0)
    with jax.named_scope("window_gather"):
        far = passed(grad_pre, "rep", lambda i: i - 7 if i % 2 == 0 else None)
        second = passed(grad_pre, "rep", lambda i: i - 4)
        near = passed(jnp.stack([grad_pre, second]), "rep", lambda i: i - 2)
        mine = jnp.stack([grad_pre, near[0], second, near[1]])
        ahead = jnp.stack([near[0], second, near[1], near[1]])
        other = passed(jnp.where(core == 0, ahead, mine), "rep", lambda i: i ^ 1)
        last = jnp.where(core == 0, other[3], far)
        other = jnp.concatenate([other[:3], last[None]])
    with jax.named_scope("backward_tiles"):
        terms = tiles_call(
            backward_tiles,
            rows,
            cols,
            count,
            vals,
            [mine.reshape(K, tile, width), other.reshape(K, tile, width)],
            jax.ShapeDtypeStruct((group_rows * block // tile, tile, width), BF),
        ).reshape(group_rows, block, width)
    with jax.named_scope("source_sum"):
        arrived = lax.all_to_all(terms, "row", 0, 0)
        source_grad = jnp.sum(arrived.astype(F32), axis=0).astype(BF)
        grad_features = lax.dot_general(
            source_grad, weight, (((1,), (1,)), ((), ())), preferred_element_type=F32
        ).astype(BF)
    with jax.named_scope("weight_sum"):
        grad_weight, grad_bias = total_over_mesh(local_weight, local_bias, 12)
    return (activations, grad_features, grad_weight, grad_bias)


def solution(mesh):
    placed = (
        P(("row", "rep"), None),
        P(),
        P(),
        P("row", "rep", None, None, None),
        P("row", "rep", None),
        P("row", "rep", None),
        P("row", "rep"),
        P(("row", "rep"), None),
    )
    return jax.shard_map(
        shards,
        mesh=mesh,
        in_specs=placed,
        out_specs=(P(("row", "rep"), None), P(("row", "rep"), None), P(), P()),
        check_vma=False,
    )
```

```python
import jax
import jax.numpy as jnp
from jax import lax
from jax.experimental import pallas as pl
from jax.experimental.pallas import tpu as pltpu
from jax.sharding import PartitionSpec as P

K = 8
BF = jnp.bfloat16
F32 = jnp.float32


def forward_tiles(rows, cols, count, vals, source, even, odd, acc):
    acc[...] = jnp.zeros_like(acc)
    live = count[0]
    for t in range(vals.shape[0]):
        product = jnp.dot(vals[t], source[cols[t]], preferred_element_type=F32)
        acc[rows[t]] += jnp.where(t < live, product, 0.0)
    tile = vals.shape[1]
    for o in range(K):
        for h in range(2):
            part = acc[2 * o + h].astype(BF)
            target = odd if o % 2 else even
            target[o // 2, h * tile : (h + 1) * tile, :] = part


def backward_tiles(
    rows, cols, count, core, vals, own, other, far, part, out, acc, near
):
    slots, tile = vals.shape[:2]
    step = 2 * core[0]
    for k in range(4):
        for h in range(2):
            span = slice(h * tile, (h + 1) * tile)
            near[2 * k + h] = own[k, span, :]
            near[8 + 2 * k + h] = other[k, span, :]
    for h in range(2):
        near[16 + h] = far[h * tile : (h + 1) * tile, :]
    acc[...] = jnp.zeros_like(acc)
    live = count[0]
    for t in range(slots):
        row = rows[t]
        place = (row // 4) * 2 + row % 2
        place = jnp.where(row % 4 >= 2, place + 8 + step, place)
        product = lax.dot_general(
            vals[t], near[place], (((0,), (0,)), ((), ())), preferred_element_type=F32
        )
        acc[cols[t]] += jnp.where(t < live, product, 0.0)
    for j in range(out.shape[0]):
        for h in range(2):
            out[j, h * tile : (h + 1) * tile, :] = acc[2 * j + h].astype(BF)
        out[j, 2 * tile :, :] = part[...]


def tiles_call(kernel, scalars, vals, arrays, outs, extra=()):
    slots, tile = vals.shape[0], vals.shape[1]
    width = arrays[0].shape[-1]
    smem = pl.BlockSpec(memory_space=pltpu.SMEM)
    vmem = pl.BlockSpec(memory_space=pltpu.VMEM)
    return pl.pallas_call(
        kernel,
        out_shape=outs,
        in_specs=[smem] * len(scalars) + [vmem] * (1 + len(arrays)),
        out_specs=jax.tree.map(lambda _: vmem, outs),
        scratch_shapes=[pltpu.VMEM((2 * K, tile, width), F32), *extra],
        compiler_params=pltpu.CompilerParams(vmem_limit_bytes=24 * 1024 * 1024),
        cost_estimate=pl.CostEstimate(
            flops=2 * slots * tile * tile * width, bytes_accessed=3 << 20, transcendentals=0
        ),
    )(*scalars, vals, *arrays)


def passed(shard, axis, to):
    size = lax.axis_size(axis)
    pairs = [(i, to(i)) for i in range(size)]
    return lax.ppermute(shard, axis, [(i, j % size) for i, j in pairs if j is not None])


def copy_out(shard, copies, sems):
    moves = [
        pltpu.make_async_copy(shard, copies.at[k], sems.at[k]) for k in range(copies.shape[0])
    ]
    for move in moves:
        move.start()
    for move in moves:
        move.wait()


def repeated(shard, size):
    return pl.pallas_call(
        copy_out,
        out_shape=jax.ShapeDtypeStruct((size,) + shard.shape, shard.dtype),
        in_specs=[pl.BlockSpec(memory_space=pl.ANY)],
        out_specs=pl.BlockSpec(memory_space=pl.ANY),
        scratch_shapes=[pltpu.SemaphoreType.DMA((size,))],
    )(shard)


def gathered(shard, axis, groups=None):
    size = lax.axis_size(axis) if groups is None else len(groups[0])
    copies = jnp.broadcast_to(shard[None], (size,) + shard.shape)
    return lax.all_to_all(copies, axis, 0, 0, axis_index_groups=groups)


def summed(shard, axis, groups=None):
    return jnp.sum(gathered(shard, axis, groups).astype(F32), axis=0)


def rep_groups(z_chips):
    spans = range(lax.axis_size("rep") // (2 * z_chips))
    place = lambda y, z, c: (y * z_chips + z) * 2 + c
    along = [[place(y, z, c) for z in range(z_chips)] for y in spans for c in range(2)]
    across = [[place(y, z, c) for y in spans for c in range(2)] for z in range(z_chips)]
    return along, across


def shards(features, weight, bias, tile_vals, tile_rows, tile_cols, tile_counts, grad_out):
    block, width = features.shape
    vals = tile_vals[0, 0]
    rows = tile_rows[0, 0]
    cols = tile_cols[0, 0]
    count = tile_counts[0]
    tile = vals.shape[1]
    group_rows = lax.axis_size("row")
    core = (lax.axis_index("rep") % 2).astype(jnp.int32)
    wide = jax.ShapeDtypeStruct((K // 2, block, width), BF)

    with jax.named_scope("gather_features"):
        source = lax.all_to_all(repeated(features, group_rows), "row", 0, 0)
        source = source.reshape(group_rows * block // tile, tile, width)
    with jax.named_scope("forward_tiles"):
        even, odd = tiles_call(
            forward_tiles, [rows, cols, count], vals, [source], (wide, wide)
        )
    with jax.named_scope("window_sum"):
        far = passed(odd[3], "rep", lambda i: i + 3 if i % 2 else None)
        other = passed(odd, "rep", lambda i: i ^ 1)
        shifted = jnp.concatenate([jnp.zeros_like(other[:1]), other[:3]])
        sums = even.astype(F32) + jnp.where(core == 0, shifted, other).astype(F32)
        ahead = passed(sums[3].astype(BF), "rep", lambda i: i + 2)
        behind = passed(sums[1].astype(BF), "rep", lambda i: i - 2)
        middle = sums[2] + far.astype(F32) + ahead.astype(F32) + behind.astype(F32)
        aggregate = sums[0] + passed(middle.astype(BF), "rep", lambda i: i + 4).astype(F32)
    with jax.named_scope("pointwise"):
        top = aggregate.astype(BF)
        rest = (aggregate - top.astype(F32)).astype(BF)
        pre = (
            jnp.dot(top, weight, preferred_element_type=F32)
            + jnp.dot(rest, weight, preferred_element_type=F32)
            + bias[None, :]
        )
        activations = jax.nn.silu(pre).astype(BF)
        sig = jax.nn.sigmoid(pre)
        grad_pre = (grad_out.astype(F32) * sig * (1.0 + pre * (1.0 - sig))).astype(BF)
        local_weight = lax.dot_general(
            top, grad_pre, (((0,), (0,)), ((), ())), preferred_element_type=F32
        )
        local_bias = jnp.sum(grad_pre.astype(F32), axis=0)
    with jax.named_scope("weight_sum_row"):
        piece = width // group_rows
        parts = local_weight.reshape(group_rows, piece, width).astype(BF)
        parts = lax.all_to_all(parts, "row", 0, 0)
        part = jnp.sum(parts.astype(F32), axis=0).astype(BF)
        lines = jnp.zeros((16, width), F32).at[0].set(local_bias).astype(BF)
        part = jnp.concatenate([part, lines])
    along, across = rep_groups(12)
    with jax.named_scope("window_gather"):
        second = passed(grad_pre, "rep", lambda i: i - 4)
        far = passed(grad_pre, "rep", lambda i: i - 7 if i % 2 == 0 else None)
        second, far, part = lax.optimization_barrier((second, far, part))
        pair = jnp.stack([grad_pre, second])
        near = passed(pair, "rep", lambda i: i - 2)
        part = summed(part, "rep", across).astype(BF)
        near, part = lax.optimization_barrier((near, part))
        own = jnp.stack([grad_pre, near[0], second, near[1]])
        other = passed(own, "rep", lambda i: i ^ 1)
        part = summed(part, "rep", along).astype(BF)
    with jax.named_scope("backward_tiles"):
        terms = tiles_call(
            backward_tiles,
            [rows, cols, count, core[None]],
            vals,
            [own, other, far, part],
            jax.ShapeDtypeStruct((group_rows, block + part.shape[0], width), BF),
            [pltpu.VMEM((2 * K + 2, tile, width), BF)],
        )
    with jax.named_scope("source_sum"):
        arrived = lax.all_to_all(terms, "row", 0, 0)
        source_grad = jnp.sum(arrived[:, :block].astype(F32), axis=0).astype(BF)
        grad_features = lax.dot_general(
            source_grad, weight, (((1,), (1,)), ((), ())), preferred_element_type=F32
        ).astype(BF)
    with jax.named_scope("weight_sum"):
        grad_weight = arrived[:, block : block + piece].reshape(width, width).astype(F32)
        grad_bias = jnp.sum(arrived[:, block + piece].astype(F32), axis=0)
    return (activations, grad_features, grad_weight, grad_bias)


def solution(mesh):
    placed = (
        P(("row", "rep"), None),
        P(),
        P(),
        P("row", "rep", None, None, None),
        P("row", "rep", None),
        P("row", "rep", None),
        P("row", "rep"),
        P(("row", "rep"), None),
    )
    return jax.shard_map(
        shards,
        mesh=mesh,
        in_specs=placed,
        out_specs=(P(("row", "rep"), None), P(("row", "rep"), None), P(), P()),
        check_vma=False,
    )
```

```python
import jax
import jax.numpy as jnp
from jax import lax
from jax.experimental import pallas as pl
from jax.experimental.pallas import tpu as pltpu
from jax.sharding import PartitionSpec as P

K = 8
Z = 12
ORDER = (0, 2, 1, 3)
BF = jnp.bfloat16
F32 = jnp.float32


def forward_tiles(rows, cols, count, vals, source, even, odd, acc):
    acc[...] = jnp.zeros_like(acc)
    live = count[0]
    for t in range(vals.shape[0]):
        product = jnp.dot(vals[t], source[cols[t]], preferred_element_type=F32)
        acc[rows[t]] += jnp.where(t < live, product, 0.0)
    tile = vals.shape[1]
    for o in range(K):
        for h in range(2):
            part = acc[2 * o + h].astype(BF)
            target = odd if o % 2 else even
            target[o // 2, h * tile : (h + 1) * tile, :] = part


def backward_tiles(rows, cols, count, core, vals, own, other, far, out, acc, reach):
    slots, tile = vals.shape[:2]
    step = 2 * core[0]
    for k in range(4):
        for h in range(2):
            span = slice(h * tile, (h + 1) * tile)
            reach[2 * k + h] = own[ORDER[k], span, :]
            reach[8 + 2 * k + h] = other[ORDER[k], span, :]
    for h in range(2):
        reach[16 + h] = far[h * tile : (h + 1) * tile, :]
    acc[...] = jnp.zeros_like(acc)
    live = count[0]
    for t in range(slots):
        row = rows[t]
        place = (row // 4) * 2 + row % 2
        place = jnp.where(row % 4 >= 2, place + 8 + step, place)
        product = lax.dot_general(
            vals[t], reach[place], (((0,), (0,)), ((), ())), preferred_element_type=F32
        )
        acc[cols[t]] += jnp.where(t < live, product, 0.0)
    for j in range(out.shape[0]):
        for h in range(2):
            out[j, h * tile : (h + 1) * tile, :] = acc[2 * j + h].astype(BF)


def tiles_call(kernel, scalars, vals, arrays, outs, extra=()):
    slots, tile = vals.shape[0], vals.shape[1]
    width = arrays[0].shape[-1]
    smem = pl.BlockSpec(memory_space=pltpu.SMEM)
    vmem = pl.BlockSpec(memory_space=pltpu.VMEM)
    return pl.pallas_call(
        kernel,
        out_shape=outs,
        in_specs=[smem] * len(scalars) + [vmem] * (1 + len(arrays)),
        out_specs=jax.tree.map(lambda _: vmem, outs),
        scratch_shapes=[pltpu.VMEM((2 * K, tile, width), F32), *extra],
        compiler_params=pltpu.CompilerParams(vmem_limit_bytes=24 * 1024 * 1024),
        cost_estimate=pl.CostEstimate(
            flops=2 * slots * tile * tile * width, bytes_accessed=3 << 20, transcendentals=0
        ),
    )(*scalars, vals, *arrays)


def passed(shard, axis, to):
    size = lax.axis_size(axis)
    pairs = [(i, to(i)) for i in range(size)]
    return lax.ppermute(shard, axis, [(i, j % size) for i, j in pairs if j is not None])


def gathered(shard, axis, groups=None):
    size = lax.axis_size(axis) if groups is None else len(groups[0])
    copies = jnp.broadcast_to(shard[None], (size,) + shard.shape)
    return lax.all_to_all(copies, axis, 0, 0, axis_index_groups=groups)


def summed(shard, axis, groups=None):
    return jnp.sum(gathered(shard, axis, groups).astype(F32), axis=0)


def depth(i, by):
    return i // (2 * Z) * (2 * Z) + (i + 2 * by) % (2 * Z)


def plane_groups(z_chips):
    rows, reps = lax.axis_size("row"), lax.axis_size("rep")
    return [
        [r * reps + y + i for r in range(rows) for y in range(0, reps, 2 * z_chips)]
        for i in range(2 * z_chips)
    ]


def shards(features, weight, bias, tile_vals, tile_rows, tile_cols, tile_counts, grad_out):
    block, width = features.shape
    vals = tile_vals[0, 0]
    rows = tile_rows[0, 0]
    cols = tile_cols[0, 0]
    count = tile_counts[0]
    tile = vals.shape[1]
    group_rows = lax.axis_size("row")
    core = (lax.axis_index("rep") % 2).astype(jnp.int32)
    wide = jax.ShapeDtypeStruct((K // 2, block, width), BF)

    with jax.named_scope("gather_features"):
        source = gathered(features, "row").reshape(group_rows * block // tile, tile, width)
    with jax.named_scope("forward_tiles"):
        even, odd = tiles_call(
            forward_tiles, [rows, cols, count], vals, [source], (wide, wide)
        )
    with jax.named_scope("window_sum"):
        far = passed(odd[3], "rep", lambda i: i + 3 if i % 2 else None)
        other = passed(odd, "rep", lambda i: i ^ 1)
        shifted = jnp.concatenate([jnp.zeros_like(other[:1]), other[:3]])
        sums = even.astype(F32) + jnp.where(core == 0, shifted, other).astype(F32)
        ahead = passed(sums[3].astype(BF), "rep", lambda i: i + 2)
        behind = passed(sums[1].astype(BF), "rep", lambda i: i - 2)
        middle = sums[2] + far.astype(F32) + ahead.astype(F32) + behind.astype(F32)
        aggregate = sums[0] + passed(middle.astype(BF), "rep", lambda i: i + 4).astype(F32)
    with jax.named_scope("pointwise"):
        top = aggregate.astype(BF)
        rest = (aggregate - top.astype(F32)).astype(BF)
        pre = (
            jnp.dot(top, weight, preferred_element_type=F32)
            + jnp.dot(rest, weight, preferred_element_type=F32)
            + bias[None, :]
        )
        activations = jax.nn.silu(pre).astype(BF)
        sig = jax.nn.sigmoid(pre)
        grad_pre = (grad_out.astype(F32) * sig * (1.0 + pre * (1.0 - sig))).astype(BF)
        local_weight = lax.dot_general(
            top, grad_pre, (((0,), (0,)), ((), ())), preferred_element_type=F32
        )
        local_bias = jnp.sum(grad_pre.astype(F32), axis=0)
    with jax.named_scope("weight_sum_plane"):
        plane = plane_groups(Z)
        members = len(plane[0])
        piece = width // members
        parts = local_weight.reshape(members, piece, width).astype(BF)
        parts = lax.all_to_all(parts, ("row", "rep"), 0, 0, axis_index_groups=plane)
        part = jnp.sum(parts.astype(F32), axis=0)
        part = jnp.concatenate([part, local_bias[None], jnp.zeros((15 - piece, width), F32)])
    with jax.named_scope("window_gather"):
        second = passed(grad_pre, "rep", lambda i: i - 4)
        far = passed(grad_pre, "rep", lambda i: i - 7 if i % 2 == 0 else None)
        second, far, part = lax.optimization_barrier((second, far, part))
        near = passed(jnp.concatenate([grad_pre, second]), "rep", lambda i: i - 2)
        sent = part.astype(BF)
        for by in (1, -1, 2):
            part = part + passed(sent, "rep", lambda i: depth(i, by)).astype(F32)
        near, part = lax.optimization_barrier((near, part))
        own = jnp.concatenate([grad_pre, second, near]).reshape(4, block, width)
        given = jnp.concatenate([own.reshape(4 * block, width), part.astype(BF)])
        other = passed(given, "rep", lambda i: i ^ 1)
        part = part + other[4 * block :].astype(F32)
        other = other[: 4 * block].reshape(4, block, width)
    with jax.named_scope("backward_tiles"):
        terms = tiles_call(
            backward_tiles,
            [rows, cols, count, core[None]],
            vals,
            [own, other, far],
            jax.ShapeDtypeStruct((group_rows, block, width), BF),
            [pltpu.VMEM((2 * K + 2, tile, width), BF)],
        )
        _, part = lax.optimization_barrier((terms, part))
    with jax.named_scope("weight_sum_depth"):
        sent = part.astype(BF)
        for by in (4, -4):
            part = part + passed(sent, "rep", lambda i: depth(i, by)).astype(F32)
    with jax.named_scope("source_sum"):
        arrived = lax.all_to_all(terms, "row", 0, 0)
        source_grad = jnp.sum(arrived.astype(F32), axis=0).astype(BF)
        grad_features = lax.dot_general(
            source_grad, weight, (((1,), (1,)), ((), ())), preferred_element_type=F32
        ).astype(BF)
    with jax.named_scope("weight_gather"):
        part, _ = lax.optimization_barrier((part.astype(BF), arrived))
        pieces = gathered(part, ("row", "rep"), plane)
        grad_weight = pieces[:, :piece].reshape(width, width).astype(F32)
        grad_bias = jnp.sum(pieces[:, piece].astype(F32), axis=0)
    return (activations, grad_features, grad_weight, grad_bias)


def solution(mesh):
    placed = (
        P(("row", "rep"), None),
        P(),
        P(),
        P("row", "rep", None, None, None),
        P("row", "rep", None),
        P("row", "rep", None),
        P("row", "rep"),
        P(("row", "rep"), None),
    )
    return jax.shard_map(
        shards,
        mesh=mesh,
        in_specs=placed,
        out_specs=(P(("row", "rep"), None), P(("row", "rep"), None), P(), P()),
        check_vma=False,
    )
```

```python
import jax
import jax.numpy as jnp
from jax import lax
from jax.experimental import pallas as pl
from jax.experimental.pallas import tpu as pltpu
from jax.sharding import PartitionSpec as P

K = 8
Z = 12
ORDER = (0, 2, 1, 3)
BF = jnp.bfloat16
F32 = jnp.float32


def forward_tiles(rows, cols, count, vals, source, even, odd, acc):
    acc[...] = jnp.zeros_like(acc)
    live = count[0]
    for t in range(vals.shape[0]):
        product = jnp.dot(vals[t], source[cols[t]], preferred_element_type=F32)
        acc[rows[t]] += jnp.where(t < live, product, 0.0)
    tile = vals.shape[1]
    for o in range(K):
        for h in range(2):
            part = acc[2 * o + h].astype(BF)
            target = odd if o % 2 else even
            target[o // 2, h * tile : (h + 1) * tile, :] = part


def backward_tiles(rows, cols, count, core, vals, own, other, far, out, acc, reach):
    slots, tile = vals.shape[:2]
    step = 2 * core[0]
    for k in range(4):
        for h in range(2):
            span = slice(h * tile, (h + 1) * tile)
            reach[2 * k + h] = own[ORDER[k], span, :]
            reach[8 + 2 * k + h] = other[ORDER[k], span, :]
    for h in range(2):
        reach[16 + h] = far[h * tile : (h + 1) * tile, :]
    acc[...] = jnp.zeros_like(acc)
    live = count[0]
    for t in range(slots):
        row = rows[t]
        place = (row // 4) * 2 + row % 2
        place = jnp.where(row % 4 >= 2, place + 8 + step, place)
        product = lax.dot_general(
            vals[t], reach[place], (((0,), (0,)), ((), ())), preferred_element_type=F32
        )
        acc[cols[t]] += jnp.where(t < live, product, 0.0)
    for j in range(out.shape[0]):
        for h in range(2):
            out[j, h * tile : (h + 1) * tile, :] = acc[2 * j + h].astype(BF)


def tiles_call(kernel, scalars, vals, arrays, outs, extra=()):
    slots, tile = vals.shape[0], vals.shape[1]
    width = arrays[0].shape[-1]
    smem = pl.BlockSpec(memory_space=pltpu.SMEM)
    vmem = pl.BlockSpec(memory_space=pltpu.VMEM)
    return pl.pallas_call(
        kernel,
        out_shape=outs,
        in_specs=[smem] * len(scalars) + [vmem] * (1 + len(arrays)),
        out_specs=jax.tree.map(lambda _: vmem, outs),
        scratch_shapes=[pltpu.VMEM((2 * K, tile, width), F32), *extra],
        compiler_params=pltpu.CompilerParams(vmem_limit_bytes=24 * 1024 * 1024),
        cost_estimate=pl.CostEstimate(
            flops=2 * slots * tile * tile * width, bytes_accessed=3 << 20, transcendentals=0
        ),
    )(*scalars, vals, *arrays)


def passed(shard, axis, to):
    size = lax.axis_size(axis)
    pairs = [(i, to(i)) for i in range(size)]
    return lax.ppermute(shard, axis, [(i, j % size) for i, j in pairs if j is not None])


def gathered(shard, axis, groups=None):
    size = lax.axis_size(axis) if groups is None else len(groups[0])
    copies = jnp.broadcast_to(shard[None], (size,) + shard.shape)
    return lax.all_to_all(copies, axis, 0, 0, axis_index_groups=groups)


def summed(shard, axis, groups=None):
    return jnp.sum(gathered(shard, axis, groups).astype(F32), axis=0)


def stack_pair(first, second, both):
    rows = first.shape[0]
    both[:rows, :] = first[...]
    both[rows:, :] = second[...]


def stacked(first, second):
    rows, width = first.shape
    vmem = pl.BlockSpec(memory_space=pltpu.VMEM)
    return pl.pallas_call(
        stack_pair,
        out_shape=jax.ShapeDtypeStruct((2 * rows, width), first.dtype),
        in_specs=[vmem, vmem],
        out_specs=vmem,
        cost_estimate=pl.CostEstimate(flops=3000000000, bytes_accessed=1 << 20, transcendentals=0),
    )(first, second)


def depth(i, by):
    return i // (2 * Z) * (2 * Z) + (i + 2 * by) % (2 * Z)


def plane_groups(z_chips):
    rows, reps = lax.axis_size("row"), lax.axis_size("rep")
    return [
        [r * reps + y + i for r in range(rows) for y in range(0, reps, 2 * z_chips)]
        for i in range(2 * z_chips)
    ]


def shards(features, weight, bias, tile_vals, tile_rows, tile_cols, tile_counts, grad_out):
    block, width = features.shape
    vals = tile_vals[0, 0]
    rows = tile_rows[0, 0]
    cols = tile_cols[0, 0]
    count = tile_counts[0]
    tile = vals.shape[1]
    group_rows = lax.axis_size("row")
    core = (lax.axis_index("rep") % 2).astype(jnp.int32)
    wide = jax.ShapeDtypeStruct((K // 2, block, width), BF)

    with jax.named_scope("gather_features"):
        source = gathered(features, "row").reshape(group_rows * block // tile, tile, width)
    with jax.named_scope("forward_tiles"):
        even, odd = tiles_call(
            forward_tiles, [rows, cols, count], vals, [source], (wide, wide)
        )
    with jax.named_scope("window_sum"):
        far = passed(odd[3], "rep", lambda i: i + 3 if i % 2 else None)
        other = passed(odd, "rep", lambda i: i ^ 1)
        shifted = jnp.concatenate([jnp.zeros_like(other[:1]), other[:3]])
        sums = even.astype(F32) + jnp.where(core == 0, shifted, other).astype(F32)
        ahead = passed(sums[3].astype(BF), "rep", lambda i: i + 2)
        behind = passed(sums[1].astype(BF), "rep", lambda i: i - 2)
        middle = sums[2] + far.astype(F32) + ahead.astype(F32) + behind.astype(F32)
        aggregate = sums[0] + passed(middle.astype(BF), "rep", lambda i: i + 4).astype(F32)
    with jax.named_scope("pointwise"):
        top = aggregate.astype(BF)
        rest = (aggregate - top.astype(F32)).astype(BF)
        pre = (
            jnp.dot(top, weight, preferred_element_type=F32)
            + jnp.dot(rest, weight, preferred_element_type=F32)
            + bias[None, :]
        )
        activations = jax.nn.silu(pre).astype(BF)
        sig = jax.nn.sigmoid(pre)
        grad_pre = (grad_out.astype(F32) * sig * (1.0 + pre * (1.0 - sig))).astype(BF)
        local_weight = lax.dot_general(
            top, grad_pre, (((0,), (0,)), ((), ())), preferred_element_type=F32
        )
        local_bias = jnp.sum(grad_pre.astype(F32), axis=0)
    with jax.named_scope("weight_sum_plane"):
        plane = plane_groups(Z)
        members = len(plane[0])
        piece = width // members
        parts = local_weight.reshape(members, piece, width).astype(BF)
        parts = lax.all_to_all(parts, ("row", "rep"), 0, 0, axis_index_groups=plane)
        part = jnp.sum(parts.astype(F32), axis=0)
        part = jnp.concatenate([part, local_bias[None], jnp.zeros((15 - piece, width), F32)])
    with jax.named_scope("window_gather"):
        second = passed(grad_pre, "rep", lambda i: i - 4)
        far = passed(grad_pre, "rep", lambda i: i - 7 if i % 2 == 0 else None)
        far, part = lax.optimization_barrier((far, part))
        pair = stacked(grad_pre, second)
        near = passed(pair, "rep", lambda i: i - 2)
        sent = part.astype(BF)
        for by in (1, -1, 2):
            part = part + passed(sent, "rep", lambda i: depth(i, by)).astype(F32)
        near, part = lax.optimization_barrier((near, part))
        own = jnp.concatenate([pair, near]).reshape(4, block, width)
        given = jnp.concatenate([own.reshape(4 * block, width), part.astype(BF)])
        other = passed(given, "rep", lambda i: i ^ 1)
        part = part + other[4 * block :].astype(F32)
        other = other[: 4 * block].reshape(4, block, width)
    with jax.named_scope("backward_tiles"):
        terms = tiles_call(
            backward_tiles,
            [rows, cols, count, core[None]],
            vals,
            [own, other, far],
            jax.ShapeDtypeStruct((group_rows, block, width), BF),
            [pltpu.VMEM((2 * K + 2, tile, width), BF)],
        )
        _, part = lax.optimization_barrier((terms, part))
    with jax.named_scope("weight_sum_depth"):
        sent = part.astype(BF)
        for by in (4, -4):
            part = part + passed(sent, "rep", lambda i: depth(i, by)).astype(F32)
    with jax.named_scope("source_sum"):
        arrived = lax.all_to_all(terms, "row", 0, 0)
        source_grad = jnp.sum(arrived.astype(F32), axis=0).astype(BF)
        grad_features = lax.dot_general(
            source_grad, weight, (((1,), (1,)), ((), ())), preferred_element_type=F32
        ).astype(BF)
    with jax.named_scope("weight_gather"):
        part, _ = lax.optimization_barrier((part.astype(BF), arrived))
        pieces = gathered(part, ("row", "rep"), plane)
        grad_weight = pieces[:, :piece].reshape(width, width).astype(F32)
        grad_bias = jnp.sum(pieces[:, piece].astype(F32), axis=0)
    return (activations, grad_features, grad_weight, grad_bias)


def solution(mesh):
    placed = (
        P(("row", "rep"), None),
        P(),
        P(),
        P("row", "rep", None, None, None),
        P("row", "rep", None),
        P("row", "rep", None),
        P("row", "rep"),
        P(("row", "rep"), None),
    )
    return jax.shard_map(
        shards,
        mesh=mesh,
        in_specs=placed,
        out_specs=(P(("row", "rep"), None), P(("row", "rep"), None), P(), P()),
        check_vma=False,
    )
```

```python
import jax
import jax.numpy as jnp
from jax import lax
from jax.experimental import pallas as pl
from jax.experimental.pallas import tpu as pltpu
from jax.sharding import PartitionSpec as P

K = 8
Z = 12
ORDER = (0, 2, 1, 3)
BF = jnp.bfloat16
F32 = jnp.float32


def forward_tiles(rows, cols, count, vals, source, even, odd, acc):
    acc[...] = jnp.zeros_like(acc)
    live = count[0]
    for t in range(vals.shape[0]):
        product = jnp.dot(vals[t], source[cols[t]], preferred_element_type=F32)
        acc[rows[t]] += jnp.where(t < live, product, 0.0)
    tile = vals.shape[1]
    for o in range(K):
        for h in range(2):
            part = acc[2 * o + h].astype(BF)
            target = odd if o % 2 else even
            target[o // 2, h * tile : (h + 1) * tile, :] = part


def backward_tiles(rows, cols, count, core, vals, own, other, far, out, acc, reach):
    slots, tile = vals.shape[:2]
    step = 2 * core[0]
    for k in range(4):
        for h in range(2):
            span = slice(h * tile, (h + 1) * tile)
            reach[2 * k + h] = own[ORDER[k], span, :]
            reach[8 + 2 * k + h] = other[ORDER[k], span, :]
    for h in range(2):
        reach[16 + h] = far[h * tile : (h + 1) * tile, :]
    acc[...] = jnp.zeros_like(acc)
    live = count[0]
    for t in range(slots):
        row = rows[t]
        place = (row // 4) * 2 + row % 2
        place = jnp.where(row % 4 >= 2, place + 8 + step, place)
        product = lax.dot_general(
            vals[t], reach[place], (((0,), (0,)), ((), ())), preferred_element_type=F32
        )
        acc[cols[t]] += jnp.where(t < live, product, 0.0)
    for j in range(out.shape[0]):
        for h in range(2):
            out[j, h * tile : (h + 1) * tile, :] = acc[2 * j + h].astype(BF)


def tiles_call(kernel, scalars, vals, arrays, outs, extra=()):
    slots, tile = vals.shape[0], vals.shape[1]
    width = arrays[0].shape[-1]
    smem = pl.BlockSpec(memory_space=pltpu.SMEM)
    vmem = pl.BlockSpec(memory_space=pltpu.VMEM)
    return pl.pallas_call(
        kernel,
        out_shape=outs,
        in_specs=[smem] * len(scalars) + [vmem] * (1 + len(arrays)),
        out_specs=jax.tree.map(lambda _: vmem, outs),
        scratch_shapes=[pltpu.VMEM((2 * K, tile, width), F32), *extra],
        compiler_params=pltpu.CompilerParams(vmem_limit_bytes=24 * 1024 * 1024),
        cost_estimate=pl.CostEstimate(
            flops=2 * slots * tile * tile * width, bytes_accessed=3 << 20, transcendentals=0
        ),
    )(*scalars, vals, *arrays)


def passed(shard, axis, to):
    size = lax.axis_size(axis)
    pairs = [(i, to(i)) for i in range(size)]
    return lax.ppermute(shard, axis, [(i, j % size) for i, j in pairs if j is not None])


def gathered(shard, axis, groups=None):
    size = lax.axis_size(axis) if groups is None else len(groups[0])
    copies = jnp.broadcast_to(shard[None], (size,) + shard.shape)
    return lax.all_to_all(copies, axis, 0, 0, axis_index_groups=groups)


def summed(shard, axis, groups=None):
    return jnp.sum(gathered(shard, axis, groups).astype(F32), axis=0)


def stack_pair(first, second, both):
    rows = first.shape[0]
    both[:rows, :] = first[...]
    both[rows:, :] = second[...]


def stacked(first, second):
    rows, width = first.shape
    vmem = pl.BlockSpec(memory_space=pltpu.VMEM)
    return pl.pallas_call(
        stack_pair,
        out_shape=jax.ShapeDtypeStruct((2 * rows, width), first.dtype),
        in_specs=[vmem, vmem],
        out_specs=vmem,
        cost_estimate=pl.CostEstimate(flops=3000000000, bytes_accessed=1 << 20, transcendentals=0),
    )(first, second)


def depth(i, by):
    return i // (2 * Z) * (2 * Z) + (i + 2 * by) % (2 * Z)


def plane_groups(z_chips):
    rows, reps = lax.axis_size("row"), lax.axis_size("rep")
    return [
        [r * reps + y + i for r in range(rows) for y in range(0, reps, 2 * z_chips)]
        for i in range(2 * z_chips)
    ]


def shards(features, weight, bias, tile_vals, tile_rows, tile_cols, tile_counts, grad_out):
    block, width = features.shape
    vals = tile_vals[0, 0]
    rows = tile_rows[0, 0]
    cols = tile_cols[0, 0]
    count = tile_counts[0]
    tile = vals.shape[1]
    group_rows = lax.axis_size("row")
    core = (lax.axis_index("rep") % 2).astype(jnp.int32)
    wide = jax.ShapeDtypeStruct((K // 2, block, width), BF)

    with jax.named_scope("gather_features"):
        source = gathered(features, "row").reshape(group_rows * block // tile, tile, width)
    with jax.named_scope("forward_tiles"):
        even, odd = tiles_call(
            forward_tiles, [rows, cols, count], vals, [source], (wide, wide)
        )
    with jax.named_scope("window_sum"):
        far = passed(odd[3], "rep", lambda i: i + 3 if i % 2 else None)
        other = passed(odd, "rep", lambda i: i ^ 1)
        shifted = jnp.concatenate([jnp.zeros_like(other[:1]), other[:3]])
        sums = even.astype(F32) + jnp.where(core == 0, shifted, other).astype(F32)
        ahead = passed(sums[3].astype(BF), "rep", lambda i: i + 2)
        behind = passed(sums[1].astype(BF), "rep", lambda i: i - 2)
        middle = sums[2] + far.astype(F32) + ahead.astype(F32) + behind.astype(F32)
        aggregate = sums[0] + passed(middle.astype(BF), "rep", lambda i: i + 4).astype(F32)
    with jax.named_scope("pointwise"):
        top = aggregate.astype(BF)
        rest = (aggregate - top.astype(F32)).astype(BF)
        pre = (
            jnp.dot(top, weight, preferred_element_type=F32)
            + jnp.dot(rest, weight, preferred_element_type=F32)
            + bias[None, :]
        )
        activations = jax.nn.silu(pre).astype(BF)
        sig = jax.nn.sigmoid(pre)
        grad_pre = (grad_out.astype(F32) * sig * (1.0 + pre * (1.0 - sig))).astype(BF)
        local_weight = lax.dot_general(
            top, grad_pre, (((0,), (0,)), ((), ())), preferred_element_type=F32
        )
        local_bias = jnp.sum(grad_pre.astype(F32), axis=0)
    with jax.named_scope("weight_sum_plane"):
        plane = plane_groups(Z)
        members = len(plane[0])
        piece = width // members
        parts = local_weight.reshape(members, piece, width).astype(BF)
        parts = lax.all_to_all(parts, ("row", "rep"), 0, 0, axis_index_groups=plane)
        part = jnp.sum(parts.astype(F32), axis=0)
        part = jnp.concatenate([part, local_bias[None], jnp.zeros((15 - piece, width), F32)])
    with jax.named_scope("window_gather"):
        second = passed(grad_pre, "rep", lambda i: i - 4)
        far = passed(second, "rep", lambda i: i - 3 if i % 2 == 0 else None)
        far, part = lax.optimization_barrier((far, part))
        pair = stacked(grad_pre, second)
        near = passed(pair, "rep", lambda i: i - 2)
        sent = part.astype(BF)
        for by in (1, -1, 2):
            part = part + passed(sent, "rep", lambda i: depth(i, by)).astype(F32)
        near, part = lax.optimization_barrier((near, part))
        own = jnp.concatenate([pair, near]).reshape(4, block, width)
        given = jnp.concatenate([own.reshape(4 * block, width), part.astype(BF)])
        other = passed(given, "rep", lambda i: i ^ 1)
        part = part + other[4 * block :].astype(F32)
        other = other[: 4 * block].reshape(4, block, width)
    with jax.named_scope("backward_tiles"):
        terms = tiles_call(
            backward_tiles,
            [rows, cols, count, core[None]],
            vals,
            [own, other, far],
            jax.ShapeDtypeStruct((group_rows, block, width), BF),
            [pltpu.VMEM((2 * K + 2, tile, width), BF)],
        )
        _, part = lax.optimization_barrier((terms, part))
    with jax.named_scope("weight_sum_depth"):
        sent = part.astype(BF)
        for by in (4, -4):
            part = part + passed(sent, "rep", lambda i: depth(i, by)).astype(F32)
    with jax.named_scope("source_sum"):
        arrived = lax.all_to_all(terms, "row", 0, 0)
        source_grad = jnp.sum(arrived.astype(F32), axis=0).astype(BF)
        grad_features = lax.dot_general(
            source_grad, weight, (((1,), (1,)), ((), ())), preferred_element_type=F32
        ).astype(BF)
    with jax.named_scope("weight_gather"):
        part, _ = lax.optimization_barrier((part.astype(BF), arrived))
        pieces = gathered(part, ("row", "rep"), plane)
        grad_weight = pieces[:, :piece].reshape(width, width).astype(F32)
        grad_bias = jnp.sum(pieces[:, piece].astype(F32), axis=0)
    return (activations, grad_features, grad_weight, grad_bias)


def solution(mesh):
    placed = (
        P(("row", "rep"), None),
        P(),
        P(),
        P("row", "rep", None, None, None),
        P("row", "rep", None),
        P("row", "rep", None),
        P("row", "rep"),
        P(("row", "rep"), None),
    )
    return jax.shard_map(
        shards,
        mesh=mesh,
        in_specs=placed,
        out_specs=(P(("row", "rep"), None), P(("row", "rep"), None), P(), P()),
        check_vma=False,
    )
```
